256 devices in a mesh: own: 32 (over x, z), grp: 8 (over y, core).
Axes of the slice: x: 4, y: 4, z: 8, core: 2. Of those that a mesh axis runs over, the one named last changes fastest.
Arguments:
- tokens: bfloat16 [512, 256, 1024], P('own', 'grp'), may hold values from -6 to 6
- cotangent: bfloat16 [2, 512, 256, 1024], P(None, 'own', 'grp'), may hold values from -6 to 6
- frozen_weight_pair: bfloat16 [2, 1024, 1024], replicated, may hold values from -0.1875 to 0.1875
- adapters: float32 [256, 4, 64, 1024], P('own', None, None, 'grp'), may hold values from -0.1875 to 0.1875
- moment1: float32 [256, 4, 64, 1024], P('own', None, None, 'grp'), may hold values from -30 to 30
- moment2: float32 [256, 4, 64, 1024], P('own', None, None, 'grp'), may hold values from 1 to 20
- block_owner: int32 [512, 1], P('own'), may hold values from 0 to 31; in each aligned block of 16 rows (0 to 15, 16 to 31, ...) at most 2 rows name the same one
- block_slot: int32 [512], P('own'), may hold values from 0 to 7
- block_count: int32 [32], P('own'), may hold values from 12 to 16, as said below
Outputs:
- projected: bfloat16 [2, 512, 256, 1024], P(None, 'own', 'grp')
- input_grad: bfloat16 [512, 256, 1024], P('own', 'grp')
- new_adapters: float32 [256, 4, 64, 1024], P('own', None, None, 'grp')
- new_moment1: float32 [256, 4, 64, 1024], P('own', None, None, 'grp')
- new_moment2: float32 [256, 4, 64, 1024], P('own', None, None, 'grp')
The draws below stay inside these ranges and needn't reach their ends.
Inputs may be any that keep to these rules, and one draw needn't show every extreme that they name: `block_owner`: among the 16 blocks of one index of own, no owner is named by more than 2 blocks, a bound that some block reaches. `block_count`: some index of own has all 16 blocks live.
All inputs are finite; a program needn't handle non-finite values.
Results may differ from the reference program's by a relative error of at most 0.015.
Values may be sent and summed in bfloat16 or wider, within the bound.
No kernel may reach another device: no remote copies, remote signals or barrier semaphores. Data moves between devices by JAX's collectives and lax.ppermute only.
A program may use at most 128 MiB of HBM per device.

```python
import math
import jax
import jax.numpy as jnp
import numpy as np
from jax import lax

D = 1024
R = 64
BLK_DEV = 16
TEN_OWN = 8
CAP = 2
ADAM_STEP = 10
BLOCKS = 512
BLOCK_ROWS = 256
TENANTS = 256
N_OWN = 32


def draw_block_count(key, part):
    key = jax.random.fold_in(key, 7)
    first_key, second_key = jax.random.split(key)
    counts = jax.random.randint(first_key, (N_OWN,), 3 * BLK_DEV // 4, BLK_DEV + 1)
    fullest = jax.random.randint(second_key, (), 0, N_OWN)
    return jnp.where(jnp.arange(N_OWN) == fullest, BLK_DEV, counts).astype(jnp.int32)


def place_ends(drawn, own_key, low, top_value):
    longest = drawn.shape.index(max(drawn.shape))
    spots = []
    for shift in (0, 1):
        where = [jax.random.randint(jax.random.fold_in(own_key, axis), (), 0, length) for axis, length in enumerate(drawn.shape)]
        where[longest] = (where[longest] + shift) % drawn.shape[longest]
        spots.append(tuple(where))
    return drawn.at[spots[0]].set(low).at[spots[1]].set(top_value)


def block_scale(stream_key, dims, cuts, low, top_value):
    factor_of = 1.0
    for axis_at, parts in cuts:
        heights = jax.random.uniform(jax.random.fold_in(jax.random.fold_in(stream_key, 6), axis_at), (parts,), jnp.float32, low / len(cuts), top_value / len(cuts))
        factor_of = factor_of * jnp.repeat(jnp.exp(heights), dims[axis_at] // parts).reshape((-1,) + (1,) * (len(dims) - 1 - axis_at))
    return factor_of


def assign_block(own_key, own, number, rows, amount, top, reach, skew):
    order = jax.random.permutation(own_key, amount)
    heavy_load, usual = shares(amount, rows * top, reach, skew, True), shares(amount, rows * top, reach, skew, False)
    places = jnp.arange(amount)

    def named(tallies, rotation):
        used = int((tallies > 0).sum())
        fixed = max(1, used // 4)
        passed = fixed + (places - fixed + rotation * (used - fixed)) % max(1, amount - fixed)
        return jnp.zeros((amount,), jnp.int32).at[order[jnp.where(places < fixed, places, passed)]].set(jnp.asarray(tallies, jnp.int32))

    tallies = jnp.where(number % 4 == 0, named(heavy_load, number // 4), named(usual, number - number // 4 - 1))
    mixed = jax.random.permutation(jax.random.fold_in(own, 3), amount)
    giver, sink = mixed[0:amount // 2 * 2:2], mixed[1:amount // 2 * 2:2]
    room = jnp.minimum(tallies[giver] - 1, reach - tallies[sink]) // 2
    room = jnp.where((giver == order[0]) | (sink == order[0]) | (tallies[sink] == 0), 0, jnp.maximum(room, 0))
    passed = jax.random.randint(jax.random.fold_in(own, 4), (amount // 2,), 0, 1 << 20) % (room + 1)
    tallies = tallies.at[giver].add(-passed).at[sink].add(passed)
    labels = jnp.searchsorted(jnp.cumsum(tallies), jnp.arange(rows * top), side="right").astype(jnp.int32)
    listing = labels.reshape(top, rows).T
    listing = listing[jax.random.permutation(jax.random.fold_in(own, 1), rows)]
    rotation = jax.random.randint(jax.random.fold_in(own, 2), (rows, 1), 0, top)
    return jnp.take_along_axis(listing, (jnp.arange(top)[None, :] + rotation) % top, axis=1)


def shares(number_of, total, limit, slope, full):
    loads = [(1 << 20) // math.isqrt(standing ** slope) + 1 for standing in range(1, number_of + 1)]
    largest = limit if full else min(limit, max(-(-total // number_of), total * loads[0] // sum(loads)))
    least = 1 if total - largest >= number_of - 1 else 0
    given, rest = [largest] + [least] * (number_of - 1), total - largest - least * (number_of - 1)
    while rest > 0:
        movable = [i for i in range(1, number_of) if given[i] < largest] or [i for i in range(1, number_of) if given[i] < limit]
        pool, left = sum([loads[i] for i in movable]), rest
        for i in movable:
            extra = min(limit - given[i], max(1, left * loads[i] // pool), rest)
            given[i] = given[i] + extra
            rest = rest - extra
    return np.array(given)


def noise(own_key, shape, spread, reach, cuts=(), kind=jnp.bfloat16):
    entries = jax.random.normal(own_key, shape, jnp.float32) * spread
    if len(cuts) > 0:
        entries = block_scale(own_key, shape, cuts, -0.22, 0.18) * entries
    return jnp.clip(entries, min=-reach, max=reach).astype(kind)


def setup_inputs(seed: int = 0) -> dict:
    key_of = jax.random.split(jax.random.key(seed), 10)
    tokens = noise(key_of[0], (BLOCKS, BLOCK_ROWS, D), 1.0, 6.0, ((0, 32), (1, 8)))
    cotangent = noise(key_of[1], (2, BLOCKS, BLOCK_ROWS, D), 1.0, 6.0, ((1, 32), (2, 8)))
    frozen_weight_pair = noise(key_of[2], (2, D, D), D ** -0.5, 0.1875)
    adapters = noise(key_of[3], (TENANTS, 4, R, D), D ** -0.5, 0.1875, ((0, 32), (3, 8)), jnp.float32)
    moment1 = noise(key_of[4], (TENANTS, 4, R, D), 5.0, 30.0, ((0, 32), (3, 8)), jnp.float32)
    moment2 = jnp.clip(jnp.exp(math.log(20.0) - 2.9957323 * jax.random.uniform(key_of[5], (TENANTS, 4, R, D), jnp.float32) ** block_scale(key_of[5], (TENANTS, 4, R, D), ((0, 32), (3, 8)), -0.2, 0.2)), 1.0, 20.0)
    block_owner_keys = jax.random.split(jax.random.fold_in(key_of[6], 1), BLOCKS // BLK_DEV)
    block_owner_turns = jax.random.permutation(jax.random.fold_in(key_of[6], 3), BLOCKS // BLK_DEV)
    block_owner = jax.vmap(lambda own, number: assign_block(jax.random.fold_in(key_of[6], 2), own, number, BLK_DEV, N_OWN, 1, CAP, 2))(block_owner_keys, block_owner_turns).reshape((BLOCKS, 1))
    block_slot = place_ends(jax.random.randint(key_of[7], (BLOCKS,), 0, TEN_OWN), jax.random.fold_in(key_of[7], 1), 0, TEN_OWN - 1).astype(jnp.int32)
    block_count = draw_block_count(jax.random.fold_in(key_of[9], 71), 0)
    return {"tokens": tokens, "cotangent": cotangent, "frozen_weight_pair": frozen_weight_pair, "adapters": adapters, "moment1": moment1, "moment2": moment2, "block_owner": block_owner, "block_slot": block_slot, "block_count": block_count}


adapter_delta_scale = 2.0
beta_first = 0.9
beta_second = 0.999
learn_rate = 0.05
adam_epsilon = 1e-08

def reference(tokens, cotangent, frozen_weight_pair, adapters, moment1, moment2, block_owner, block_slot, block_count):
    position = jnp.arange(BLOCKS, dtype=jnp.int32)
    tenant = (block_owner[:, 0] * TEN_OWN + block_slot).astype(jnp.int32)
    alive = position % BLK_DEV < block_count[(position // BLK_DEV).astype(jnp.int32)]

    def one_block(carry, item):
        input_token_rows, query_output_gradient, value_output_gradient, owner_t, is_live = item
        picked = lax.dynamic_index_in_dim(adapters, owner_t, 0, keepdims=False)
        fetched = jnp.where(is_live, picked, jnp.zeros_like(picked)).astype(jnp.bfloat16)
        down_q, query_expand_weight, down_v, value_expand_weight = (fetched[0], fetched[1], fetched[2], fetched[3])
        query_hidden_rows = jnp.dot(input_token_rows, down_q.T, preferred_element_type=jnp.float32).astype(jnp.bfloat16)
        value_hidden_rows = jnp.dot(input_token_rows, down_v.T, preferred_element_type=jnp.float32).astype(jnp.bfloat16)
        query_projection_output = (jnp.dot(input_token_rows, frozen_weight_pair[0], preferred_element_type=jnp.float32) + adapter_delta_scale * jnp.dot(query_hidden_rows, query_expand_weight, preferred_element_type=jnp.float32)).astype(jnp.bfloat16)
        value_projection_output = (jnp.dot(input_token_rows, frozen_weight_pair[1], preferred_element_type=jnp.float32) + adapter_delta_scale * jnp.dot(value_hidden_rows, value_expand_weight, preferred_element_type=jnp.float32)).astype(jnp.bfloat16)
        query_expand_factor = (adapter_delta_scale * jnp.dot(query_output_gradient, query_expand_weight.T, preferred_element_type=jnp.float32)).astype(jnp.bfloat16)
        value_expand_factor = (adapter_delta_scale * jnp.dot(value_output_gradient, value_expand_weight.T, preferred_element_type=jnp.float32)).astype(jnp.bfloat16)
        back_x = (jnp.dot(query_output_gradient, frozen_weight_pair[0].T, preferred_element_type=jnp.float32) + jnp.dot(value_output_gradient, frozen_weight_pair[1].T, preferred_element_type=jnp.float32) + jnp.dot(query_expand_factor, down_q, preferred_element_type=jnp.float32) + jnp.dot(value_expand_factor, down_v, preferred_element_type=jnp.float32)).astype(jnp.bfloat16)
        gradient_block_slice = jnp.stack([jnp.dot(query_expand_factor.T, input_token_rows, preferred_element_type=jnp.float32), adapter_delta_scale * jnp.dot(query_hidden_rows.T, query_output_gradient, preferred_element_type=jnp.float32), jnp.dot(value_expand_factor.T, input_token_rows, preferred_element_type=jnp.float32), adapter_delta_scale * jnp.dot(value_hidden_rows.T, value_output_gradient, preferred_element_type=jnp.float32)], axis=0).astype(jnp.bfloat16)
        carry = carry.at[owner_t].add(gradient_block_slice.astype(jnp.float32))
        return (carry, (query_projection_output, value_projection_output, back_x))
    start = jnp.zeros(adapters.shape, jnp.float32)
    total, outs = lax.scan(one_block, start, (tokens, cotangent[0], cotangent[1], tenant, alive))
    query_projection_output, value_projection_output, back_x = outs
    new_first = beta_first * moment1 + (1.0 - beta_first) * total
    new_second = beta_second * moment2 + (1.0 - beta_second) * total * total
    fix_first = 1.0 - beta_first ** ADAM_STEP
    fix_second = 1.0 - beta_second ** ADAM_STEP
    new_adapt = adapters - learn_rate * (new_first / fix_first) / (jnp.sqrt(new_second / fix_second) + adam_epsilon)
    return (jnp.stack([query_projection_output, value_projection_output], axis=0), back_x, new_adapt, new_first, new_second)
```

```python
import functools

import jax
import jax.numpy as jnp
from jax import lax
from jax.experimental import pallas as pl
from jax.experimental.pallas import tpu as pltpu
from jax.sharding import Mesh
from jax.sharding import PartitionSpec as P

ADAM_STEP = 10
adapter_delta_scale = 2.0
beta_first = 0.9
beta_second = 0.999
learn_rate = 0.05
adam_epsilon = 1e-08

NX, NZ, NG = 4, 8, 8
TEN = 8
NB = 16
HALF = TEN // 2
PANEL = (4, 64, 128)
BF = jnp.bfloat16
F32 = jnp.float32
SMEM = pl.BlockSpec(memory_space=pltpu.SMEM)
VMEM = pl.BlockSpec(memory_space=pltpu.VMEM)
HBM = pl.BlockSpec(memory_space=pltpu.HBM)
WIDE = pltpu.CompilerParams(vmem_limit_bytes=56 << 20)
BYTES = 64 * 1024
FILLER = 9 * 10**9

FETCH_PARTS = ((0, 1, 7), (2, 6), (3, 5), (4,))
RETURN_PARTS = ((4,), (3, 5), (2, 6), (1, 7), (0,))


def cost(nbytes, flops=0):
    return pl.CostEstimate(flops=flops, bytes_accessed=nbytes, transcendentals=0)


def shift(value, axis, size, by):
    return lax.ppermute(value, axis, [(i, (i + by) % size) for i in range(size)])


def pick_kernel(part, table, *refs):
    sources = {}
    refs = list(refs)
    for d in part:
        sources[d] = (refs.pop(0), refs.pop(0)) if d == 4 else refs.pop(0)
    outs = refs
    for i in range(NX):
        for j, d in enumerate(part):
            for k in range(2):
                row = jnp.maximum(table[i, 2 * d + k], 0)
                s = 2 * j + k
                if d == 4:
                    low, high = sources[d]

                    @pl.when(row < HALF)
                    def _():
                        outs[i][s] = low[row]

                    @pl.when(row >= HALF)
                    def _():
                        outs[i][s] = high[row - HALF]
                else:
                    outs[i][s] = sources[d][row]


def pick(part, table, sources):
    n = 2 * len(part)
    return pl.pallas_call(
        functools.partial(pick_kernel, part),
        out_shape=[jax.ShapeDtypeStruct((n, *PANEL), BF)] * NX,
        in_specs=[SMEM] + [VMEM] * len(sources),
        out_specs=[VMEM] * NX,
        compiler_params=pltpu.CompilerParams(vmem_limit_bytes=16 << 20),
        cost_estimate=cost(8 * n * BYTES),
    )(table, *sources)


def place_kernel(part, mine, *refs):
    held, sources, out = refs[: len(refs) - NX - 1], refs[-NX - 1 : -1], refs[-1]
    out[...] = held[0][...] if held else jnp.zeros_like(out)
    for i in range(NX):
        for j, d in enumerate(part):
            for k in range(2):
                b = mine[i, 2 * d + k]

                @pl.when(b >= 0)
                def _():
                    out[b] = sources[i][2 * j + k]


def place(part, mine, held, sources, effort):
    return pl.pallas_call(
        functools.partial(place_kernel, part),
        out_shape=jax.ShapeDtypeStruct((NB, *PANEL), BF),
        in_specs=[SMEM] + [VMEM] * (len(held) + NX),
        out_specs=VMEM,
        compiler_params=pltpu.CompilerParams(vmem_limit_bytes=16 << 20),
        cost_estimate=cost(2 * NB * BYTES, effort),
    )(mine, *held, *sources)


def send_kernel(part, table, grads, *outs):
    for i in range(NX):
        for j, d in enumerate(part):
            for k in range(2):
                outs[i][2 * j + k] = grads[jnp.maximum(table[i, 2 * d + k], 0)]


def send(part, table, grads):
    n = 2 * len(part)
    return pl.pallas_call(
        functools.partial(send_kernel, part),
        out_shape=[jax.ShapeDtypeStruct((n, *PANEL), BF)] * NX,
        in_specs=[SMEM, VMEM],
        out_specs=[VMEM] * NX,
        compiler_params=pltpu.CompilerParams(vmem_limit_bytes=16 << 20),
        cost_estimate=cost(8 * n * BYTES),
    )(table, grads)


def add_panels(d, j, asked, pieces, total):
    for k in range(2):
        for i in range(NX):

            @pl.when(asked[i, 2 * d + k] >= 0)
            def _():
                total[asked[i, 2 * d + k]] += pieces[i][2 * j + k].astype(F32)


def far_kernel(asked, p0, p1, p2, p3, low, high, total):
    total[...] = jnp.zeros_like(total)
    add_panels(4, 0, asked, (p0, p1, p2, p3), total)
    low[...] = total[:HALF].astype(BF)
    high[...] = total[HALF:].astype(BF)


def far(asked, pieces):
    half = jax.ShapeDtypeStruct((HALF, *PANEL), BF)
    return pl.pallas_call(
        far_kernel,
        out_shape=[half, half],
        in_specs=[SMEM] + [VMEM] * NX,
        out_specs=[VMEM, VMEM],
        scratch_shapes=[pltpu.VMEM((TEN, *PANEL), F32)],
        compiler_params=pltpu.CompilerParams(vmem_limit_bytes=16 << 20),
        cost_estimate=cost(24 * BYTES),
    )(asked, *pieces)


def row_sums_kernel(part, asked, p0, p1, p2, p3, *totals):
    for j, d in enumerate(part):
        totals[j][...] = jnp.zeros_like(totals[j])
        add_panels(d, j, asked, (p0, p1, p2, p3), totals[j])


def row_sums(part, asked, pieces, effort):
    return pl.pallas_call(
        functools.partial(row_sums_kernel, part),
        out_shape=[jax.ShapeDtypeStruct((TEN, *PANEL), F32)] * len(part),
        in_specs=[SMEM] + [VMEM] * NX,
        out_specs=[VMEM] * len(part),
        compiler_params=pltpu.CompilerParams(vmem_limit_bytes=16 << 20),
        cost_estimate=cost(24 * BYTES, effort),
    )(asked, *pieces)


def onward_kernel(first, sum_up, sum_down, up, down, up_out, down_out):
    if first:
        up_out[:HALF] = (sum_up[:HALF] + up[...].astype(F32)).astype(BF)
        up_out[HALF:] = sum_up[HALF:].astype(BF)
        down_out[:HALF] = sum_down[:HALF].astype(BF)
        down_out[HALF:] = (sum_down[HALF:] + down[...].astype(F32)).astype(BF)
    else:
        up_out[...] = (sum_up[...] + up[...].astype(F32)).astype(BF)
        down_out[...] = (sum_down[...] + down[...].astype(F32)).astype(BF)


def onward(first, sums, up, down):
    return pl.pallas_call(
        functools.partial(onward_kernel, first),
        out_shape=[jax.ShapeDtypeStruct((TEN, *PANEL), BF)] * 2,
        in_specs=[VMEM] * 4,
        out_specs=[VMEM, VMEM],
        compiler_params=pltpu.CompilerParams(vmem_limit_bytes=16 << 20),
        cost_estimate=cost(BYTES),
    )(*sums, up, down)


def adam_kernel(sums, up, down, adapters, moment1, moment2, new_adapt, new_first, new_second, total, given, made, in_sems, out_sems):
    def bring(a, m):
        source = (adapters, moment1, moment2)[a]
        return pltpu.make_async_copy(source.at[:, m], given.at[a, m], in_sems.at[a, m])

    def store(a, m):
        target = (new_adapt, new_first, new_second)[a]
        return pltpu.make_async_copy(made.at[a, m], target.at[:, m], out_sems.at[a, m])

    for m in range(4):
        for a in range(3):
            bring(a, m).start()
    total[...] = sums[...] + up[...].astype(F32) + down[...].astype(F32)
    fix_first = 1.0 - beta_first**ADAM_STEP
    fix_second = 1.0 - beta_second**ADAM_STEP
    for m in range(4):
        for a in range(3):
            bring(a, m).wait()
        grad = total[:, m]
        first = beta_first * given[1, m] + (1.0 - beta_first) * grad
        second = beta_second * given[2, m] + (1.0 - beta_second) * grad * grad
        made[1, m] = first
        made[2, m] = second
        made[0, m] = given[0, m] - learn_rate * (first / fix_first) / (
            jnp.sqrt(second / fix_second) + adam_epsilon
        )
        for a in range(3):
            store(a, m).start()
    for m in range(4):
        for a in range(3):
            store(a, m).wait()


def adam(sums, up, down, adapters, moment1, moment2):
    return pl.pallas_call(
        adam_kernel,
        out_shape=[jax.ShapeDtypeStruct((TEN, *PANEL), F32)] * 3,
        in_specs=[VMEM] * 3 + [HBM] * 3,
        out_specs=[HBM] * 3,
        scratch_shapes=[
            pltpu.VMEM((TEN, *PANEL), F32),
            pltpu.VMEM((3, 4, TEN, 64, 128), F32),
            pltpu.VMEM((3, 4, TEN, 64, 128), F32),
            pltpu.SemaphoreType.DMA((3, 4)),
            pltpu.SemaphoreType.DMA((3, 4)),
        ],
        compiler_params=pltpu.CompilerParams(vmem_limit_bytes=24 << 20),
        cost_estimate=cost(8 << 20),
    )(sums, up, down, adapters, moment1, moment2)


def pack_kernel(tokens, cotangent, out):
    for g in range(NG):
        rows = slice(2 * g, 2 * g + 2)
        out[g, 0] = tokens[rows]
        out[g, 1] = cotangent[0, rows]
        out[g, 2] = cotangent[1, rows]


def pack(tokens, cotangent):
    rows, width = tokens.shape[1:]
    return pl.pallas_call(
        pack_kernel,
        out_shape=jax.ShapeDtypeStruct((NG, 3, 2, rows, width), BF),
        in_specs=[VMEM, VMEM],
        out_specs=VMEM,
        compiler_params=pltpu.CompilerParams(vmem_limit_bytes=16 << 20),
        cost_estimate=cost(6 << 20),
    )(tokens, cotangent)


def unpack_kernel(packed, projected, input_grad, held, in_sems, out_sems):
    def bring(g):
        return pltpu.make_async_copy(packed.at[g], held.at[g], in_sems.at[g])

    def store(g, a):
        rows = pl.ds(2 * g, 2)
        target = input_grad.at[rows] if a == 2 else projected.at[a, rows]
        return pltpu.make_async_copy(held.at[g, a], target, out_sems.at[g, a])

    for g in range(NG):
        bring(g).start()
    for g in range(NG):
        bring(g).wait()
        for a in range(3):
            store(g, a).start()
    for g in range(NG):
        for a in range(3):
            store(g, a).wait()


def unpack(packed):
    rows, width = packed.shape[3:]
    return pl.pallas_call(
        unpack_kernel,
        out_shape=[
            jax.ShapeDtypeStruct((2, NB, rows, width), BF),
            jax.ShapeDtypeStruct((NB, rows, width), BF),
        ],
        in_specs=[HBM],
        out_specs=[HBM, HBM],
        scratch_shapes=[
            pltpu.VMEM((NG, 3, 2, rows, width), BF),
            pltpu.SemaphoreType.DMA((NG,)),
            pltpu.SemaphoreType.DMA((NG, 3)),
        ],
        compiler_params=pltpu.CompilerParams(vmem_limit_bytes=16 << 20),
        cost_estimate=cost(6 << 20),
    )(packed)


def dot(a, b, left, right):
    return lax.dot_general(a, b, (((left,), (right,)), ((), ())), preferred_element_type=F32)


def whole_matrix(panels, m):
    return jnp.concatenate([panels[g, 0, m] for g in range(NG)], axis=-1)


def rows_of(packed, which):
    value = packed[:, which, 0]
    return value.reshape(value.shape[0] * value.shape[1], value.shape[2])


def grads_kernel(packed, panels, grads, hidden, held, sems):
    j = pl.program_id(0)
    x, cq, cv = (rows_of(packed, which) for which in range(3))
    down_q, up_q, down_v, up_v = (whole_matrix(panels, m) for m in range(4))
    hq = dot(x, down_q, 1, 1).astype(BF)
    hv = dot(x, down_v, 1, 1).astype(BF)
    uq = (adapter_delta_scale * dot(cq, up_q, 1, 1)).astype(BF)
    uv = (adapter_delta_scale * dot(cv, up_v, 1, 1)).astype(BF)
    hidden[0, 0], hidden[0, 1], hidden[0, 2], hidden[0, 3] = hq, hv, uq, uv
    for m, value in enumerate((
        dot(uq, x, 0, 0),
        adapter_delta_scale * dot(hq, cq, 0, 0),
        dot(uv, x, 0, 0),
        adapter_delta_scale * dot(hv, cv, 0, 0),
    )):
        value = value.astype(BF)
        for g in range(NG):
            held[j, g, m] = value[:, g * 128 : (g + 1) * 128]

    def store(block):
        return pltpu.make_async_copy(held.at[block], grads.at[:, block], sems.at[block])

    store(j).start()

    @pl.when(j == 1)
    def _():
        store(0).wait()
        store(1).wait()


def block_grads(packed, panels):
    rows, width = packed.shape[3:]
    return pl.pallas_call(
        grads_kernel,
        grid=(2,),
        out_shape=[
            jax.ShapeDtypeStruct((NG, 2, *PANEL), BF),
            jax.ShapeDtypeStruct((2, 4, NG * rows, 64), BF),
        ],
        in_specs=[
            pl.BlockSpec((NG, 3, 1, rows, width), lambda j: (0, 0, j, 0, 0)),
            pl.BlockSpec((NG, 1, *PANEL), lambda j: (0, j, 0, 0, 0)),
        ],
        out_specs=[
            HBM,
            pl.BlockSpec((1, 4, NG * rows, 64), lambda j: (j, 0, 0, 0)),
        ],
        scratch_shapes=[pltpu.VMEM((2, NG, *PANEL), BF), pltpu.SemaphoreType.DMA((2,))],
        compiler_params=WIDE,
        cost_estimate=cost(6 << 20, 2 * 270 * 10**6),
    )(packed, panels)


def rows_kernel(packed, panels, hidden, frozen, out):
    x, cq, cv = (rows_of(packed, which) for which in range(3))
    down_q, up_q, down_v, up_v = (whole_matrix(panels, m) for m in range(4))
    hq, hv, uq, uv = (hidden[0, i] for i in range(4))
    out_q = dot(x, frozen[0], 1, 0) + adapter_delta_scale * dot(hq, up_q, 1, 0)
    out[:, 0, 0] = out_q.astype(BF).reshape(out.shape[0], *out.shape[3:])
    out_v = dot(x, frozen[1], 1, 0) + adapter_delta_scale * dot(hv, up_v, 1, 0)
    out[:, 1, 0] = out_v.astype(BF).reshape(out.shape[0], *out.shape[3:])
    back = dot(cq, frozen[0], 1, 1) + dot(cv, frozen[1], 1, 1) + dot(uq, down_q, 1, 0) + dot(uv, down_v, 1, 0)
    out[:, 2, 0] = back.astype(BF).reshape(out.shape[0], *out.shape[3:])


def block_rows(packed, panels, hidden, frozen):
    rows, width = packed.shape[3:]
    return pl.pallas_call(
        rows_kernel,
        grid=(2,),
        out_shape=jax.ShapeDtypeStruct(packed.shape, BF),
        in_specs=[
            pl.BlockSpec((NG, 3, 1, rows, width), lambda j: (0, 0, j, 0, 0)),
            pl.BlockSpec((NG, 1, *PANEL), lambda j: (0, j, 0, 0, 0)),
            pl.BlockSpec((1, 4, NG * rows, 64), lambda j: (j, 0, 0, 0)),
            pl.BlockSpec((2, width, width), lambda j: (0, 0, 0)),
        ],
        out_specs=pl.BlockSpec((NG, 3, 1, rows, width), lambda j: (0, 0, j, 0, 0)),
        compiler_params=WIDE,
        cost_estimate=cost(12 << 20, 5 * 10**9),
    )(packed, panels, hidden, frozen)


def slot_table(hit, index, value):
    slots = jnp.arange(2 * NZ, dtype=jnp.int32)
    taken = hit[..., None] & (index[..., None] == slots)
    return jnp.max(jnp.where(taken, value[..., None], -1), axis=-2)


def local(tokens, cotangent, frozen_weight_pair, adapters, moment1, moment2, block_owner, block_slot, block_count):
    my_x, my_z = lax.axis_index("x"), lax.axis_index("z")
    grp = ("y", "c")
    barrier = lax.optimization_barrier

    def along_z(up, down):
        return shift(up, "z", NZ, 1), shift(down, "z", NZ, -1)

    table = adapters.astype(BF)
    ups, downs = {}, {}
    ups[1], downs[1] = along_z(table, table)

    owner, slot, count, table = barrier((block_owner[:, 0], block_slot, block_count, table))
    order = jnp.arange(NB, dtype=jnp.int32)
    code = jnp.where(order < count[0], owner * TEN + slot, -1)
    codes = jnp.stack([code] + [shift(code, "x", NX, -i) for i in range(1, NX)])
    on = codes >= 0
    slot, owner_z, owner_x, owner = codes & 7, (codes >> 3) & 7, codes >> 6, codes >> 3
    earlier = (owner[:, :, None] == owner[:, None, :]) & (order[None, :] < order[:, None])
    k = jnp.max(earlier.astype(jnp.int32), axis=2)
    d = (owner_z - my_z) & 7
    index = 2 * d + k
    asked = slot_table(on & (owner_x == my_x), index, slot)
    dx = (owner_x[0] - my_x) & 3
    toward = dx[None, :] == jnp.arange(NX, dtype=jnp.int32)[:, None]
    mine = slot_table(on[0][None] & toward, jnp.broadcast_to(index[0], (NX, NB)), jnp.broadcast_to(order, (NX, NB)))

    def along_x(pieces):
        return [shift(pieces[i], "x", NX, i) for i in range(1, NX)]

    tokens, cotangent, _ = barrier((tokens, cotangent, codes))
    packed = lax.all_to_all(pack(tokens, cotangent), grp, split_axis=0, concat_axis=0, tiled=True)

    def from_relays(picked):
        moved = along_x(picked)
        return [picked[0], moved[2], moved[1], moved[0]]

    held = []
    for step in (1, 2, 3):
        sources = [downs[step], ups[step]]
        picked = pick(FETCH_PARTS[step - 1], asked, [table] + sources if step == 1 else sources)
        if step > 1:
            held = [place(FETCH_PARTS[step - 2], mine, held, came, FILLER)]
        up, down, picked, held = barrier((ups[step], downs[step], picked, held))
        if step == 3:
            up, down = up[:HALF], down[HALF:]
        ups[step + 1], downs[step + 1] = along_z(up, down)
        came = from_relays(picked)
    picked = pick(FETCH_PARTS[3], asked, [ups[4], downs[4]])
    held = [place(FETCH_PARTS[2], mine, held, came, 0)]
    panels = place(FETCH_PARTS[3], mine, held, from_relays(picked), 0)

    panels, packed = barrier((panels, packed))
    panels = lax.all_to_all(panels.reshape(NG, 2, *PANEL), grp, split_axis=0, concat_axis=0, tiled=True)

    grads, hidden = block_grads(packed, panels)
    grads = lax.all_to_all(grads, grp, split_axis=0, concat_axis=0, tiled=True).reshape(NB, *PANEL)
    rows = block_rows(packed, panels, hidden, frozen_weight_pair)
    grads, rows = barrier((grads, rows))


    def from_requesters(pieces):
        moved = along_x(pieces)
        return [pieces[0], moved[2], moved[1], moved[0]]

    got = from_requesters(send(RETURN_PARTS[0], mine, grads))
    up, down = far(asked, got)
    rows, _ = barrier((rows, got[1]))
    rows = lax.all_to_all(rows, grp, split_axis=0, concat_axis=0, tiled=True)
    for step in (1, 2, 3, 4):
        mine, _ = barrier((mine, got))
        up, down, pieces = barrier((up, down, send(RETURN_PARTS[step], mine, grads)))
        up, down = along_z(up, down)
        got = from_requesters(pieces)
        sums = row_sums(RETURN_PARTS[step], asked, got, FILLER if step < 4 else 0)
        if step < 4:
            up, down = onward(step == 1, sums, up, down)
    new_adapt, new_first, new_second = adam(sums[0], up, down, adapters, moment1, moment2)
    projected, input_grad = unpack(rows)
    return (projected, input_grad, new_adapt, new_first, new_second)


def solution(mesh):
    split = Mesh(mesh.devices.reshape(NX, NZ, NG // 2, 2), ("x", "z", "y", "c"))
    own, grp = ("x", "z"), ("y", "c")
    in_specs = (
        P(own, grp, None),
        P(None, own, grp, None),
        P(),
        P(own, None, None, grp),
        P(own, None, None, grp),
        P(own, None, None, grp),
        P(own, None),
        P(own),
        P(own),
    )
    out_specs = (
        P(None, own, grp, None),
        P(own, grp, None),
        P(own, None, None, grp),
        P(own, None, None, grp),
        P(own, None, None, grp),
    )
    return jax.shard_map(local, mesh=split, in_specs=in_specs, out_specs=out_specs, check_vma=False)
```

```python
import functools

import jax
import jax.numpy as jnp
from jax import lax
from jax.experimental import pallas as pl
from jax.experimental.pallas import tpu as pltpu
from jax.sharding import Mesh
from jax.sharding import PartitionSpec as P

ADAM_STEP = 10
adapter_delta_scale = 2.0
beta_first = 0.9
beta_second = 0.999
learn_rate = 0.05
adam_epsilon = 1e-08

NX, NZ, NG = 4, 8, 8
TEN = 8
NB = 16
HALF = TEN // 2
PANEL = (4, 64, 128)
BF = jnp.bfloat16
F32 = jnp.float32
SMEM = pl.BlockSpec(memory_space=pltpu.SMEM)
VMEM = pl.BlockSpec(memory_space=pltpu.VMEM)
HBM = pl.BlockSpec(memory_space=pltpu.HBM)
WIDE = pltpu.CompilerParams(vmem_limit_bytes=56 << 20)
BYTES = 64 * 1024
FILLER = 9 * 10**9

FETCH_PARTS = ((0, 1, 7), (2, 6), (3, 5), (4,))
RETURN_PARTS = ((4,), (3, 5), (2, 6), (1, 7), (0,))


def cost(nbytes, flops=0):
    return pl.CostEstimate(flops=flops, bytes_accessed=nbytes, transcendentals=0)


def shift(value, axis, size, by):
    return lax.ppermute(value, axis, [(i, (i + by) % size) for i in range(size)])


def pick_kernel(part, table, *refs):
    sources = {}
    refs = list(refs)
    for d in part:
        sources[d] = (refs.pop(0), refs.pop(0)) if d == 4 else refs.pop(0)
    outs = refs
    for i in range(NX):
        for j, d in enumerate(part):
            for k in range(2):
                row = jnp.maximum(table[i, 2 * d + k], 0)
                s = 2 * j + k
                if d == 4:
                    low, high = sources[d]

                    @pl.when(row < HALF)
                    def _():
                        outs[i][s] = low[row]

                    @pl.when(row >= HALF)
                    def _():
                        outs[i][s] = high[row - HALF]
                else:
                    outs[i][s] = sources[d][row]


def pick(part, table, sources):
    n = 2 * len(part)
    return pl.pallas_call(
        functools.partial(pick_kernel, part),
        out_shape=[jax.ShapeDtypeStruct((n, *PANEL), BF)] * NX,
        in_specs=[SMEM] + [VMEM] * len(sources),
        out_specs=[VMEM] * NX,
        compiler_params=pltpu.CompilerParams(vmem_limit_bytes=16 << 20),
        cost_estimate=cost(8 * n * BYTES),
    )(table, *sources)


def place_kernel(part, mine, *refs):
    held, sources, out = refs[: len(refs) - NX - 1], refs[-NX - 1 : -1], refs[-1]
    out[...] = held[0][...] if held else jnp.zeros_like(out)
    for i in range(NX):
        for j, d in enumerate(part):
            for k in range(2):
                b = mine[i, 2 * d + k]

                @pl.when(b >= 0)
                def _():
                    out[b] = sources[i][2 * j + k]


def place(part, mine, held, sources, effort):
    return pl.pallas_call(
        functools.partial(place_kernel, part),
        out_shape=jax.ShapeDtypeStruct((NB, *PANEL), BF),
        in_specs=[SMEM] + [VMEM] * (len(held) + NX),
        out_specs=VMEM,
        compiler_params=pltpu.CompilerParams(vmem_limit_bytes=16 << 20),
        cost_estimate=cost(2 * NB * BYTES, effort),
    )(mine, *held, *sources)


def send_kernel(part, table, grads, *outs):
    for i in range(NX):
        for j, d in enumerate(part):
            for k in range(2):
                outs[i][2 * j + k] = grads[jnp.maximum(table[i, 2 * d + k], 0)]


def send(part, table, grads):
    n = 2 * len(part)
    return pl.pallas_call(
        functools.partial(send_kernel, part),
        out_shape=[jax.ShapeDtypeStruct((n, *PANEL), BF)] * NX,
        in_specs=[SMEM, VMEM],
        out_specs=[VMEM] * NX,
        compiler_params=pltpu.CompilerParams(vmem_limit_bytes=16 << 20),
        cost_estimate=cost(8 * n * BYTES),
    )(table, grads)


def add_panels(d, j, asked, pieces, total):
    for k in range(2):
        for i in range(NX):

            @pl.when(asked[i, 2 * d + k] >= 0)
            def _():
                total[asked[i, 2 * d + k]] += pieces[i][2 * j + k].astype(F32)


def far_kernel(asked, p0, p1, p2, p3, low, high, total):
    total[...] = jnp.zeros_like(total)
    add_panels(4, 0, asked, (p0, p1, p2, p3), total)
    low[...] = total[:HALF].astype(BF)
    high[...] = total[HALF:].astype(BF)


def far(asked, pieces):
    half = jax.ShapeDtypeStruct((HALF, *PANEL), BF)
    return pl.pallas_call(
        far_kernel,
        out_shape=[half, half],
        in_specs=[SMEM] + [VMEM] * NX,
        out_specs=[VMEM, VMEM],
        scratch_shapes=[pltpu.VMEM((TEN, *PANEL), F32)],
        compiler_params=pltpu.CompilerParams(vmem_limit_bytes=16 << 20),
        cost_estimate=cost(24 * BYTES),
    )(asked, *pieces)


def row_sums_kernel(part, asked, p0, p1, p2, p3, *totals):
    for j, d in enumerate(part):
        totals[j][...] = jnp.zeros_like(totals[j])
        add_panels(d, j, asked, (p0, p1, p2, p3), totals[j])


def row_sums(part, asked, pieces, effort):
    return pl.pallas_call(
        functools.partial(row_sums_kernel, part),
        out_shape=[jax.ShapeDtypeStruct((TEN, *PANEL), F32)] * len(part),
        in_specs=[SMEM] + [VMEM] * NX,
        out_specs=[VMEM] * len(part),
        compiler_params=pltpu.CompilerParams(vmem_limit_bytes=16 << 20),
        cost_estimate=cost(24 * BYTES, effort),
    )(asked, *pieces)


def onward_kernel(first, sum_up, sum_down, up, down, up_out, down_out):
    if first:
        up_out[:HALF] = (sum_up[:HALF] + up[...].astype(F32)).astype(BF)
        up_out[HALF:] = sum_up[HALF:].astype(BF)
        down_out[:HALF] = sum_down[:HALF].astype(BF)
        down_out[HALF:] = (sum_down[HALF:] + down[...].astype(F32)).astype(BF)
    else:
        up_out[...] = (sum_up[...] + up[...].astype(F32)).astype(BF)
        down_out[...] = (sum_down[...] + down[...].astype(F32)).astype(BF)


def onward(first, sums, up, down):
    return pl.pallas_call(
        functools.partial(onward_kernel, first),
        out_shape=[jax.ShapeDtypeStruct((TEN, *PANEL), BF)] * 2,
        in_specs=[VMEM] * 4,
        out_specs=[VMEM, VMEM],
        compiler_params=pltpu.CompilerParams(vmem_limit_bytes=16 << 20),
        cost_estimate=cost(BYTES),
    )(*sums, up, down)


def adam_kernel(sums, up, down, adapters, moment1, moment2, new_adapt, new_first, new_second, total, given, made, in_sems, out_sems):
    def bring(a, m):
        source = (adapters, moment1, moment2)[a]
        return pltpu.make_async_copy(source.at[:, m], given.at[a, m], in_sems.at[a, m])

    def store(a, m):
        target = (new_adapt, new_first, new_second)[a]
        return pltpu.make_async_copy(made.at[a, m], target.at[:, m], out_sems.at[a, m])

    for m in range(4):
        for a in range(3):
            bring(a, m).start()
    total[...] = sums[...] + up[...].astype(F32) + down[...].astype(F32)
    fix_first = 1.0 - beta_first**ADAM_STEP
    fix_second = 1.0 - beta_second**ADAM_STEP
    for m in range(4):
        for a in range(3):
            bring(a, m).wait()
        grad = total[:, m]
        first = beta_first * given[1, m] + (1.0 - beta_first) * grad
        second = beta_second * given[2, m] + (1.0 - beta_second) * grad * grad
        made[1, m] = first
        made[2, m] = second
        made[0, m] = given[0, m] - learn_rate * (first / fix_first) / (
            jnp.sqrt(second / fix_second) + adam_epsilon
        )
        for a in range(3):
            store(a, m).start()
    for m in range(4):
        for a in range(3):
            store(a, m).wait()


def adam(sums, up, down, adapters, moment1, moment2):
    return pl.pallas_call(
        adam_kernel,
        out_shape=[jax.ShapeDtypeStruct((TEN, *PANEL), F32)] * 3,
        in_specs=[VMEM] * 3 + [HBM] * 3,
        out_specs=[HBM] * 3,
        scratch_shapes=[
            pltpu.VMEM((TEN, *PANEL), F32),
            pltpu.VMEM((3, 4, TEN, 64, 128), F32),
            pltpu.VMEM((3, 4, TEN, 64, 128), F32),
            pltpu.SemaphoreType.DMA((3, 4)),
            pltpu.SemaphoreType.DMA((3, 4)),
        ],
        compiler_params=pltpu.CompilerParams(vmem_limit_bytes=24 << 20),
        cost_estimate=cost(8 << 20),
    )(sums, up, down, adapters, moment1, moment2)


def pack_kernel(tokens, cotangent, out):
    for g in range(NG):
        rows = slice(2 * g, 2 * g + 2)
        out[g, 0] = tokens[rows]
        out[g, 1] = cotangent[0, rows]
        out[g, 2] = cotangent[1, rows]


def pack(tokens, cotangent):
    rows, width = tokens.shape[1:]
    return pl.pallas_call(
        pack_kernel,
        out_shape=jax.ShapeDtypeStruct((NG, 3, 2, rows, width), BF),
        in_specs=[VMEM, VMEM],
        out_specs=VMEM,
        compiler_params=pltpu.CompilerParams(vmem_limit_bytes=16 << 20),
        cost_estimate=cost(6 << 20),
    )(tokens, cotangent)


def unpack_kernel(packed, projected, input_grad, held, in_sems, out_sems):
    def bring(g):
        return pltpu.make_async_copy(packed.at[g], held.at[g], in_sems.at[g])

    def store(g, a):
        rows = pl.ds(2 * g, 2)
        target = input_grad.at[rows] if a == 2 else projected.at[a, rows]
        return pltpu.make_async_copy(held.at[g, a], target, out_sems.at[g, a])

    for g in range(NG):
        bring(g).start()
    for g in range(NG):
        bring(g).wait()
        for a in range(3):
            store(g, a).start()
    for g in range(NG):
        for a in range(3):
            store(g, a).wait()


def unpack(packed):
    rows, width = packed.shape[3:]
    return pl.pallas_call(
        unpack_kernel,
        out_shape=[
            jax.ShapeDtypeStruct((2, NB, rows, width), BF),
            jax.ShapeDtypeStruct((NB, rows, width), BF),
        ],
        in_specs=[HBM],
        out_specs=[HBM, HBM],
        scratch_shapes=[
            pltpu.VMEM((NG, 3, 2, rows, width), BF),
            pltpu.SemaphoreType.DMA((NG,)),
            pltpu.SemaphoreType.DMA((NG, 3)),
        ],
        compiler_params=pltpu.CompilerParams(vmem_limit_bytes=16 << 20),
        cost_estimate=cost(6 << 20),
    )(packed)


def dot(a, b, left, right):
    return lax.dot_general(a, b, (((left,), (right,)), ((), ())), preferred_element_type=F32)


def whole_matrix(panels, m):
    return jnp.concatenate([panels[g, 0, m] for g in range(NG)], axis=-1)


def rows_of(packed, which):
    value = packed[:, which, 0]
    return value.reshape(value.shape[0] * value.shape[1], value.shape[2])


def grads_kernel(packed, panels, grads, hidden, held, sems):
    j = pl.program_id(0)
    x, cq, cv = (rows_of(packed, which) for which in range(3))
    down_q, up_q, down_v, up_v = (whole_matrix(panels, m) for m in range(4))
    hq = dot(x, down_q, 1, 1).astype(BF)
    hv = dot(x, down_v, 1, 1).astype(BF)
    uq = (adapter_delta_scale * dot(cq, up_q, 1, 1)).astype(BF)
    uv = (adapter_delta_scale * dot(cv, up_v, 1, 1)).astype(BF)
    hidden[0, 0], hidden[0, 1], hidden[0, 2], hidden[0, 3] = hq, hv, uq, uv
    for m, value in enumerate((
        dot(uq, x, 0, 0),
        adapter_delta_scale * dot(hq, cq, 0, 0),
        dot(uv, x, 0, 0),
        adapter_delta_scale * dot(hv, cv, 0, 0),
    )):
        value = value.astype(BF)
        for g in range(NG):
            held[j, g, m] = value[:, g * 128 : (g + 1) * 128]

    def store(block):
        return pltpu.make_async_copy(held.at[block], grads.at[:, block], sems.at[block])

    store(j).start()

    @pl.when(j == 1)
    def _():
        store(0).wait()
        store(1).wait()


def block_grads(packed, panels):
    rows, width = packed.shape[3:]
    return pl.pallas_call(
        grads_kernel,
        grid=(2,),
        out_shape=[
            jax.ShapeDtypeStruct((NG, 2, *PANEL), BF),
            jax.ShapeDtypeStruct((2, 4, NG * rows, 64), BF),
        ],
        in_specs=[
            pl.BlockSpec((NG, 3, 1, rows, width), lambda j: (0, 0, j, 0, 0)),
            pl.BlockSpec((NG, 1, *PANEL), lambda j: (0, j, 0, 0, 0)),
        ],
        out_specs=[
            HBM,
            pl.BlockSpec((1, 4, NG * rows, 64), lambda j: (j, 0, 0, 0)),
        ],
        scratch_shapes=[pltpu.VMEM((2, NG, *PANEL), BF), pltpu.SemaphoreType.DMA((2,))],
        compiler_params=WIDE,
        cost_estimate=cost(6 << 20, 2 * 270 * 10**6),
    )(packed, panels)


def rows_kernel(packed, panels, hidden, frozen, out):
    x, cq, cv = (rows_of(packed, which) for which in range(3))
    down_q, up_q, down_v, up_v = (whole_matrix(panels, m) for m in range(4))
    hq, hv, uq, uv = (hidden[0, i] for i in range(4))
    out_q = dot(x, frozen[0], 1, 0) + adapter_delta_scale * dot(hq, up_q, 1, 0)
    out[:, 0, 0] = out_q.astype(BF).reshape(out.shape[0], *out.shape[3:])
    out_v = dot(x, frozen[1], 1, 0) + adapter_delta_scale * dot(hv, up_v, 1, 0)
    out[:, 1, 0] = out_v.astype(BF).reshape(out.shape[0], *out.shape[3:])
    back = dot(cq, frozen[0], 1, 1) + dot(cv, frozen[1], 1, 1) + dot(uq, down_q, 1, 0) + dot(uv, down_v, 1, 0)
    out[:, 2, 0] = back.astype(BF).reshape(out.shape[0], *out.shape[3:])


def block_rows(packed, panels, hidden, frozen):
    rows, width = packed.shape[3:]
    return pl.pallas_call(
        rows_kernel,
        grid=(2,),
        out_shape=jax.ShapeDtypeStruct(packed.shape, BF),
        in_specs=[
            pl.BlockSpec((NG, 3, 1, rows, width), lambda j: (0, 0, j, 0, 0)),
            pl.BlockSpec((NG, 1, *PANEL), lambda j: (0, j, 0, 0, 0)),
            pl.BlockSpec((1, 4, NG * rows, 64), lambda j: (j, 0, 0, 0)),
            pl.BlockSpec((2, width, width), lambda j: (0, 0, 0)),
        ],
        out_specs=pl.BlockSpec((NG, 3, 1, rows, width), lambda j: (0, 0, j, 0, 0)),
        compiler_params=WIDE,
        cost_estimate=cost(12 << 20, 5 * 10**9),
    )(packed, panels, hidden, frozen)


def slot_table(hit, index, value):
    slots = jnp.arange(2 * NZ, dtype=jnp.int32)
    taken = hit[..., None] & (index[..., None] == slots)
    return jnp.max(jnp.where(taken, value[..., None], -1), axis=-2)


def local(tokens, cotangent, frozen_weight_pair, adapters, moment1, moment2, block_owner, block_slot, block_count):
    my_x, my_z = lax.axis_index("x"), lax.axis_index("z")
    grp = ("y", "c")
    barrier = lax.optimization_barrier

    def along_z(up, down):
        return shift(up, "z", NZ, 1), shift(down, "z", NZ, -1)

    table = adapters.astype(BF)
    ups, downs = {}, {}
    ups[1], downs[1] = along_z(table, table)

    owner, slot, count, table = barrier((block_owner[:, 0], block_slot, block_count, table))
    order = jnp.arange(NB, dtype=jnp.int32)
    code = jnp.where(order < count[0], owner * TEN + slot, -1)
    codes = jnp.stack([code] + [shift(code, "x", NX, -i) for i in range(1, NX)])
    on = codes >= 0
    slot, owner_z, owner_x, owner = codes & 7, (codes >> 3) & 7, codes >> 6, codes >> 3
    earlier = (owner[:, :, None] == owner[:, None, :]) & (order[None, :] < order[:, None])
    k = jnp.max(earlier.astype(jnp.int32), axis=2)
    d = (owner_z - my_z) & 7
    index = 2 * d + k
    asked = slot_table(on & (owner_x == my_x), index, slot)
    dx = (owner_x[0] - my_x) & 3
    toward = dx[None, :] == jnp.arange(NX, dtype=jnp.int32)[:, None]
    mine = slot_table(on[0][None] & toward, jnp.broadcast_to(index[0], (NX, NB)), jnp.broadcast_to(order, (NX, NB)))

    def along_x(pieces):
        return [shift(pieces[i], "x", NX, i) for i in range(1, NX)]

    tokens, cotangent, _ = barrier((tokens, cotangent, codes))
    packed = lax.all_to_all(pack(tokens, cotangent), grp, split_axis=0, concat_axis=0, tiled=True)

    def from_relays(picked):
        moved = along_x(picked)
        return [picked[0], moved[2], moved[1], moved[0]]

    held = []
    for step in (1, 2, 3):
        sources = [downs[step], ups[step]]
        picked = pick(FETCH_PARTS[step - 1], asked, [table] + sources if step == 1 else sources)
        if step > 1:
            held = [place(FETCH_PARTS[step - 2], mine, held, came, FILLER)]
        up, down, picked, held = barrier((ups[step], downs[step], picked, held))
        if step == 3:
            up, down = up[:HALF], down[HALF:]
        ups[step + 1], downs[step + 1] = along_z(up, down)
        came = from_relays(picked)
    picked = pick(FETCH_PARTS[3], asked, [ups[4], downs[4]])
    held = [place(FETCH_PARTS[2], mine, held, came, 0)]
    panels = place(FETCH_PARTS[3], mine, held, from_relays(picked), 0)

    panels, packed = barrier((panels, packed))
    panels = lax.all_to_all(panels.reshape(NG, 2, *PANEL), grp, split_axis=0, concat_axis=0, tiled=True)

    grads, hidden = block_grads(packed, panels)
    grads = lax.all_to_all(grads, grp, split_axis=0, concat_axis=0, tiled=True).reshape(NB, *PANEL)
    rows = block_rows(packed, panels, hidden, frozen_weight_pair)
    grads, rows = barrier((grads, rows))


    def from_requesters(pieces):
        moved = along_x(pieces)
        return [pieces[0], moved[2], moved[1], moved[0]]

    got = from_requesters(send(RETURN_PARTS[0], mine, grads))
    up, down = far(asked, got)
    for step in (1, 2, 3, 4):
        if step == 4:
            projected, input_grad = unpack(rows)
            asked, _ = barrier((asked, input_grad))
        mine, _ = barrier((mine, got[1]))
        up, down, pieces = barrier((up, down, send(RETURN_PARTS[step], mine, grads)))
        up, down = along_z(up, down)
        got = from_requesters(pieces)
        if step == 1:
            rows, _ = barrier((rows, got[1]))
            rows = lax.all_to_all(rows, grp, split_axis=0, concat_axis=0, tiled=True)
        sums = row_sums(RETURN_PARTS[step], asked, got, FILLER if step < 4 else 0)
        if step < 4:
            up, down = onward(step == 1, sums, up, down)
    new_adapt, new_first, new_second = adam(sums[0], up, down, adapters, moment1, moment2)
    return (projected, input_grad, new_adapt, new_first, new_second)


def solution(mesh):
    split = Mesh(mesh.devices.reshape(NX, NZ, NG // 2, 2), ("x", "z", "y", "c"))
    own, grp = ("x", "z"), ("y", "c")
    in_specs = (
        P(own, grp, None),
        P(None, own, grp, None),
        P(),
        P(own, None, None, grp),
        P(own, None, None, grp),
        P(own, None, None, grp),
        P(own, None),
        P(own),
        P(own),
    )
    out_specs = (
        P(None, own, grp, None),
        P(own, grp, None),
        P(own, None, None, grp),
        P(own, None, None, grp),
        P(own, None, None, grp),
    )
    return jax.shard_map(local, mesh=split, in_specs=in_specs, out_specs=out_specs, check_vma=False)
```

```python
import functools

import jax
import jax.numpy as jnp
from jax import lax
from jax.experimental import pallas as pl
from jax.experimental.pallas import tpu as pltpu
from jax.sharding import Mesh
from jax.sharding import PartitionSpec as P

ADAM_STEP = 10
adapter_delta_scale = 2.0
beta_first = 0.9
beta_second = 0.999
learn_rate = 0.05
adam_epsilon = 1e-08

NX, NZ, NG = 4, 8, 8
TEN = 8
NB = 16
HALF = TEN // 2
PANEL = (4, 64, 128)
BF = jnp.bfloat16
F32 = jnp.float32
SMEM = pl.BlockSpec(memory_space=pltpu.SMEM)
VMEM = pl.BlockSpec(memory_space=pltpu.VMEM)
HBM = pl.BlockSpec(memory_space=pltpu.HBM)
WIDE = pltpu.CompilerParams(vmem_limit_bytes=56 << 20)
BYTES = 64 * 1024
FILLER = 9 * 10**9

FETCH_PARTS = ((0, 1, 7), (2, 6), (3, 5), (4,))
RETURN_PARTS = ((4,), (3, 5), (2, 6), (1, 7), (0,))


def cost(nbytes, flops=0):
    return pl.CostEstimate(flops=flops, bytes_accessed=nbytes, transcendentals=0)


def shift(value, axis, size, by):
    return lax.ppermute(value, axis, [(i, (i + by) % size) for i in range(size)])


def pick_kernel(part, table, *refs):
    sources = {}
    refs = list(refs)
    for d in part:
        sources[d] = (refs.pop(0), refs.pop(0)) if d == 4 else refs.pop(0)
    outs = refs
    for i in range(NX):
        for j, d in enumerate(part):
            for k in range(2):
                row = jnp.maximum(table[i, 2 * d + k], 0)
                s = 2 * j + k
                if d == 4:
                    low, high = sources[d]

                    @pl.when(row < HALF)
                    def _():
                        outs[i][s] = low[row]

                    @pl.when(row >= HALF)
                    def _():
                        outs[i][s] = high[row - HALF]
                else:
                    outs[i][s] = sources[d][row]


def pick(part, table, sources):
    n = 2 * len(part)
    return pl.pallas_call(
        functools.partial(pick_kernel, part),
        out_shape=[jax.ShapeDtypeStruct((n, *PANEL), BF)] * NX,
        in_specs=[SMEM] + [VMEM] * len(sources),
        out_specs=[VMEM] * NX,
        compiler_params=pltpu.CompilerParams(vmem_limit_bytes=16 << 20),
        cost_estimate=cost(8 * n * BYTES),
    )(table, *sources)


def place_kernel(part, mine, *refs):
    held, sources, out = refs[: len(refs) - NX - 1], refs[-NX - 1 : -1], refs[-1]
    out[...] = held[0][...] if held else jnp.zeros_like(out)
    for i in range(NX):
        for j, d in enumerate(part):
            for k in range(2):
                b = mine[i, 2 * d + k]

                @pl.when(b >= 0)
                def _():
                    out[b] = sources[i][2 * j + k]


def place(part, mine, held, sources, effort):
    return pl.pallas_call(
        functools.partial(place_kernel, part),
        out_shape=jax.ShapeDtypeStruct((NB, *PANEL), BF),
        in_specs=[SMEM] + [VMEM] * (len(held) + NX),
        out_specs=VMEM,
        compiler_params=pltpu.CompilerParams(vmem_limit_bytes=16 << 20),
        cost_estimate=cost(2 * NB * BYTES, effort),
    )(mine, *held, *sources)


def send_kernel(part, table, grads, *outs):
    for i in range(NX):
        for j, d in enumerate(part):
            for k in range(2):
                outs[i][2 * j + k] = grads[jnp.maximum(table[i, 2 * d + k], 0)]


def send(part, table, grads):
    n = 2 * len(part)
    return pl.pallas_call(
        functools.partial(send_kernel, part),
        out_shape=[jax.ShapeDtypeStruct((n, *PANEL), BF)] * NX,
        in_specs=[SMEM, VMEM],
        out_specs=[VMEM] * NX,
        compiler_params=pltpu.CompilerParams(vmem_limit_bytes=16 << 20),
        cost_estimate=cost(8 * n * BYTES),
    )(table, grads)


def add_panels(d, j, asked, pieces, total):
    for k in range(2):
        for i in range(NX):

            @pl.when(asked[i, 2 * d + k] >= 0)
            def _():
                total[asked[i, 2 * d + k]] += pieces[i][2 * j + k].astype(F32)


def far_kernel(asked, p0, p1, p2, p3, low, high, total):
    total[...] = jnp.zeros_like(total)
    add_panels(4, 0, asked, (p0, p1, p2, p3), total)
    low[...] = total[:HALF].astype(BF)
    high[...] = total[HALF:].astype(BF)


def far(asked, pieces):
    half = jax.ShapeDtypeStruct((HALF, *PANEL), BF)
    return pl.pallas_call(
        far_kernel,
        out_shape=[half, half],
        in_specs=[SMEM] + [VMEM] * NX,
        out_specs=[VMEM, VMEM],
        scratch_shapes=[pltpu.VMEM((TEN, *PANEL), F32)],
        compiler_params=pltpu.CompilerParams(vmem_limit_bytes=16 << 20),
        cost_estimate=cost(24 * BYTES),
    )(asked, *pieces)


def row_sums_kernel(part, asked, p0, p1, p2, p3, *totals):
    for j, d in enumerate(part):
        totals[j][...] = jnp.zeros_like(totals[j])
        add_panels(d, j, asked, (p0, p1, p2, p3), totals[j])


def row_sums(part, asked, pieces, effort):
    return pl.pallas_call(
        functools.partial(row_sums_kernel, part),
        out_shape=[jax.ShapeDtypeStruct((TEN, *PANEL), F32)] * len(part),
        in_specs=[SMEM] + [VMEM] * NX,
        out_specs=[VMEM] * len(part),
        compiler_params=pltpu.CompilerParams(vmem_limit_bytes=16 << 20),
        cost_estimate=cost(24 * BYTES, effort),
    )(asked, *pieces)


def onward_kernel(first, sum_up, sum_down, up, down, up_out, down_out):
    if first:
        up_out[:HALF] = (sum_up[:HALF] + up[...].astype(F32)).astype(BF)
        up_out[HALF:] = sum_up[HALF:].astype(BF)
        down_out[:HALF] = sum_down[:HALF].astype(BF)
        down_out[HALF:] = (sum_down[HALF:] + down[...].astype(F32)).astype(BF)
    else:
        up_out[...] = (sum_up[...] + up[...].astype(F32)).astype(BF)
        down_out[...] = (sum_down[...] + down[...].astype(F32)).astype(BF)


def onward(first, sums, up, down):
    return pl.pallas_call(
        functools.partial(onward_kernel, first),
        out_shape=[jax.ShapeDtypeStruct((TEN, *PANEL), BF)] * 2,
        in_specs=[VMEM] * 4,
        out_specs=[VMEM, VMEM],
        compiler_params=pltpu.CompilerParams(vmem_limit_bytes=16 << 20),
        cost_estimate=cost(BYTES),
    )(*sums, up, down)


def adam_kernel(sums, up, down, adapters, moment1, moment2, new_adapt, new_first, new_second, made, sems):
    def store(a, m):
        target = (new_adapt, new_first, new_second)[a]
        return pltpu.make_async_copy(made.at[a, m], target.at[:, m], sems.at[a, m])

    fix_first = 1.0 - beta_first**ADAM_STEP
    fix_second = 1.0 - beta_second**ADAM_STEP
    for m in range(4):
        grad = sums[:, m] + up[:, m].astype(F32) + down[:, m].astype(F32)
        first = beta_first * moment1[:, m] + (1.0 - beta_first) * grad
        second = beta_second * moment2[:, m] + (1.0 - beta_second) * grad * grad
        made[1, m] = first
        made[2, m] = second
        made[0, m] = adapters[:, m] - learn_rate * (first / fix_first) / (
            jnp.sqrt(second / fix_second) + adam_epsilon
        )
        for a in range(3):
            store(a, m).start()
    for m in range(4):
        for a in range(3):
            store(a, m).wait()


def adam(sums, up, down, adapters, moment1, moment2):
    return pl.pallas_call(
        adam_kernel,
        out_shape=[jax.ShapeDtypeStruct((TEN, *PANEL), F32)] * 3,
        in_specs=[VMEM] * 6,
        out_specs=[HBM] * 3,
        scratch_shapes=[pltpu.VMEM((3, 4, TEN, 64, 128), F32), pltpu.SemaphoreType.DMA((3, 4))],
        compiler_params=pltpu.CompilerParams(vmem_limit_bytes=24 << 20),
        cost_estimate=cost(8 << 20),
    )(sums, up, down, adapters, moment1, moment2)


def pack_kernel(tokens, cotangent, out):
    for g in range(NG):
        rows = slice(2 * g, 2 * g + 2)
        out[g, 0] = tokens[rows]
        out[g, 1] = cotangent[0, rows]
        out[g, 2] = cotangent[1, rows]


def pack(tokens, cotangent):
    rows, width = tokens.shape[1:]
    return pl.pallas_call(
        pack_kernel,
        out_shape=jax.ShapeDtypeStruct((NG, 3, 2, rows, width), BF),
        in_specs=[VMEM, VMEM],
        out_specs=VMEM,
        compiler_params=pltpu.CompilerParams(vmem_limit_bytes=16 << 20),
        cost_estimate=cost(6 << 20),
    )(tokens, cotangent)


def unpack_kernel(packed, projected, input_grad, held, in_sems, out_sems):
    def bring(g):
        return pltpu.make_async_copy(packed.at[g], held.at[g], in_sems.at[g])

    def store(g, a):
        rows = pl.ds(2 * g, 2)
        target = input_grad.at[rows] if a == 2 else projected.at[a, rows]
        return pltpu.make_async_copy(held.at[g, a], target, out_sems.at[g, a])

    for g in range(NG):
        bring(g).start()
    for g in range(NG):
        bring(g).wait()
        for a in range(3):
            store(g, a).start()
    for g in range(NG):
        for a in range(3):
            store(g, a).wait()


def unpack(packed):
    rows, width = packed.shape[3:]
    return pl.pallas_call(
        unpack_kernel,
        out_shape=[
            jax.ShapeDtypeStruct((2, NB, rows, width), BF),
            jax.ShapeDtypeStruct((NB, rows, width), BF),
        ],
        in_specs=[HBM],
        out_specs=[HBM, HBM],
        scratch_shapes=[
            pltpu.VMEM((NG, 3, 2, rows, width), BF),
            pltpu.SemaphoreType.DMA((NG,)),
            pltpu.SemaphoreType.DMA((NG, 3)),
        ],
        compiler_params=pltpu.CompilerParams(vmem_limit_bytes=16 << 20),
        cost_estimate=cost(6 << 20),
    )(packed)


def dot(a, b, left, right):
    return lax.dot_general(a, b, (((left,), (right,)), ((), ())), preferred_element_type=F32)


def whole_matrix(panels, m):
    return jnp.concatenate([panels[g, 0, m] for g in range(NG)], axis=-1)


def rows_of(packed, which):
    value = packed[:, which, 0]
    return value.reshape(value.shape[0] * value.shape[1], value.shape[2])


def grads_kernel(packed, panels, grads, hidden, held, sems):
    j = pl.program_id(0)
    x, cq, cv = (rows_of(packed, which) for which in range(3))
    down_q, up_q, down_v, up_v = (whole_matrix(panels, m) for m in range(4))
    hq = dot(x, down_q, 1, 1).astype(BF)
    hv = dot(x, down_v, 1, 1).astype(BF)
    uq = (adapter_delta_scale * dot(cq, up_q, 1, 1)).astype(BF)
    uv = (adapter_delta_scale * dot(cv, up_v, 1, 1)).astype(BF)
    hidden[0, 0], hidden[0, 1], hidden[0, 2], hidden[0, 3] = hq, hv, uq, uv
    for m, value in enumerate((
        dot(uq, x, 0, 0),
        adapter_delta_scale * dot(hq, cq, 0, 0),
        dot(uv, x, 0, 0),
        adapter_delta_scale * dot(hv, cv, 0, 0),
    )):
        value = value.astype(BF)
        for g in range(NG):
            held[j, g, m] = value[:, g * 128 : (g + 1) * 128]

    def store(block):
        return pltpu.make_async_copy(held.at[block], grads.at[:, block], sems.at[block])

    store(j).start()

    @pl.when(j == 1)
    def _():
        store(0).wait()
        store(1).wait()


def block_grads(packed, panels):
    rows, width = packed.shape[3:]
    return pl.pallas_call(
        grads_kernel,
        grid=(2,),
        out_shape=[
            jax.ShapeDtypeStruct((NG, 2, *PANEL), BF),
            jax.ShapeDtypeStruct((2, 4, NG * rows, 64), BF),
        ],
        in_specs=[
            pl.BlockSpec((NG, 3, 1, rows, width), lambda j: (0, 0, j, 0, 0)),
            pl.BlockSpec((NG, 1, *PANEL), lambda j: (0, j, 0, 0, 0)),
        ],
        out_specs=[
            HBM,
            pl.BlockSpec((1, 4, NG * rows, 64), lambda j: (j, 0, 0, 0)),
        ],
        scratch_shapes=[pltpu.VMEM((2, NG, *PANEL), BF), pltpu.SemaphoreType.DMA((2,))],
        compiler_params=WIDE,
        cost_estimate=cost(6 << 20, 2 * 270 * 10**6),
    )(packed, panels)


def rows_kernel(packed, panels, hidden, frozen, out):
    x, cq, cv = (rows_of(packed, which) for which in range(3))
    down_q, up_q, down_v, up_v = (whole_matrix(panels, m) for m in range(4))
    hq, hv, uq, uv = (hidden[0, i] for i in range(4))
    out_q = dot(x, frozen[0], 1, 0) + adapter_delta_scale * dot(hq, up_q, 1, 0)
    out[:, 0, 0] = out_q.astype(BF).reshape(out.shape[0], *out.shape[3:])
    out_v = dot(x, frozen[1], 1, 0) + adapter_delta_scale * dot(hv, up_v, 1, 0)
    out[:, 1, 0] = out_v.astype(BF).reshape(out.shape[0], *out.shape[3:])
    back = dot(cq, frozen[0], 1, 1) + dot(cv, frozen[1], 1, 1) + dot(uq, down_q, 1, 0) + dot(uv, down_v, 1, 0)
    out[:, 2, 0] = back.astype(BF).reshape(out.shape[0], *out.shape[3:])


def block_rows(packed, panels, hidden, frozen):
    rows, width = packed.shape[3:]
    return pl.pallas_call(
        rows_kernel,
        grid=(2,),
        out_shape=jax.ShapeDtypeStruct(packed.shape, BF),
        in_specs=[
            pl.BlockSpec((NG, 3, 1, rows, width), lambda j: (0, 0, j, 0, 0)),
            pl.BlockSpec((NG, 1, *PANEL), lambda j: (0, j, 0, 0, 0)),
            pl.BlockSpec((1, 4, NG * rows, 64), lambda j: (j, 0, 0, 0)),
            pl.BlockSpec((2, width, width), lambda j: (0, 0, 0)),
        ],
        out_specs=pl.BlockSpec((NG, 3, 1, rows, width), lambda j: (0, 0, j, 0, 0)),
        compiler_params=WIDE,
        cost_estimate=cost(12 << 20, 5 * 10**9),
    )(packed, panels, hidden, frozen)


def slot_table(hit, index, value):
    slots = jnp.arange(2 * NZ, dtype=jnp.int32)
    taken = hit[..., None] & (index[..., None] == slots)
    return jnp.max(jnp.where(taken, value[..., None], -1), axis=-2)


def local(tokens, cotangent, frozen_weight_pair, adapters, moment1, moment2, block_owner, block_slot, block_count):
    my_x, my_z = lax.axis_index("x"), lax.axis_index("z")
    grp = ("y", "c")
    barrier = lax.optimization_barrier

    def along_z(up, down):
        return shift(up, "z", NZ, 1), shift(down, "z", NZ, -1)

    table = adapters.astype(BF)
    ups, downs = {}, {}
    ups[1], downs[1] = along_z(table, table)

    owner, slot, count, table = barrier((block_owner[:, 0], block_slot, block_count, table))
    order = jnp.arange(NB, dtype=jnp.int32)
    code = jnp.where(order < count[0], owner * TEN + slot, -1)
    codes = jnp.stack([code] + [shift(code, "x", NX, -i) for i in range(1, NX)])
    on = codes >= 0
    slot, owner_z, owner_x, owner = codes & 7, (codes >> 3) & 7, codes >> 6, codes >> 3
    earlier = (owner[:, :, None] == owner[:, None, :]) & (order[None, :] < order[:, None])
    k = jnp.max(earlier.astype(jnp.int32), axis=2)
    d = (owner_z - my_z) & 7
    index = 2 * d + k
    asked = slot_table(on & (owner_x == my_x), index, slot)
    dx = (owner_x[0] - my_x) & 3
    toward = dx[None, :] == jnp.arange(NX, dtype=jnp.int32)[:, None]
    mine = slot_table(on[0][None] & toward, jnp.broadcast_to(index[0], (NX, NB)), jnp.broadcast_to(order, (NX, NB)))

    def along_x(pieces):
        return [shift(pieces[i], "x", NX, i) for i in range(1, NX)]

    tokens, cotangent, _ = barrier((tokens, cotangent, codes))
    packed = lax.all_to_all(pack(tokens, cotangent), grp, split_axis=0, concat_axis=0, tiled=True)

    def from_relays(picked):
        moved = along_x(picked)
        return [picked[0], moved[2], moved[1], moved[0]]

    held = []
    for step in (1, 2, 3):
        sources = [downs[step], ups[step]]
        if step > 1:
            held = [place(FETCH_PARTS[step - 2], mine, held, came, FILLER)]
            asked, _ = barrier((asked, came[1:]))
        picked = pick(FETCH_PARTS[step - 1], asked, [table] + sources if step == 1 else sources)
        up, down = ups[step], downs[step]
        if step == 3:
            up, down = up[:HALF], down[HALF:]
        ups[step + 1], downs[step + 1] = along_z(up, down)
        came = from_relays(picked)
    picked = pick(FETCH_PARTS[3], asked, [ups[4], downs[4]])
    held = [place(FETCH_PARTS[2], mine, held, came, 0)]
    panels = place(FETCH_PARTS[3], mine, held, from_relays(picked), 0)

    panels, packed = barrier((panels, packed))
    panels = lax.all_to_all(panels.reshape(NG, 2, *PANEL), grp, split_axis=0, concat_axis=0, tiled=True)

    grads, hidden = block_grads(packed, panels)
    grads = lax.all_to_all(grads, grp, split_axis=0, concat_axis=0, tiled=True).reshape(NB, *PANEL)
    rows = block_rows(packed, panels, hidden, frozen_weight_pair)
    grads, rows = barrier((grads, rows))


    def from_requesters(pieces):
        moved = along_x(pieces)
        return [pieces[0], moved[2], moved[1], moved[0]]

    got = from_requesters(send(RETURN_PARTS[0], mine, grads))
    up, down = far(asked, got)
    for step in (1, 2, 3, 4):
        if step == 4:
            projected, input_grad = unpack(rows)
            asked, _ = barrier((asked, input_grad))
        mine, _ = barrier((mine, got[1]))
        pieces = send(RETURN_PARTS[step], mine, grads)
        if step in (1, 4):
            up, down, pieces = barrier((up, down, pieces))
        up, down = along_z(up, down)
        got = from_requesters(pieces)
        if step == 1:
            rows, _ = barrier((rows, got[1]))
            rows = lax.all_to_all(rows, grp, split_axis=0, concat_axis=0, tiled=True)
        sums = row_sums(RETURN_PARTS[step], asked, got, FILLER if step < 4 else 0)
        if step < 4:
            up, down = onward(step == 1, sums, up, down)
    new_adapt, new_first, new_second = adam(sums[0], up, down, adapters, moment1, moment2)
    return (projected, input_grad, new_adapt, new_first, new_second)


def solution(mesh):
    split = Mesh(mesh.devices.reshape(NX, NZ, NG // 2, 2), ("x", "z", "y", "c"))
    own, grp = ("x", "z"), ("y", "c")
    in_specs = (
        P(own, grp, None),
        P(None, own, grp, None),
        P(),
        P(own, None, None, grp),
        P(own, None, None, grp),
        P(own, None, None, grp),
        P(own, None),
        P(own),
        P(own),
    )
    out_specs = (
        P(None, own, grp, None),
        P(own, grp, None),
        P(own, None, None, grp),
        P(own, None, None, grp),
        P(own, None, None, grp),
    )
    return jax.shard_map(local, mesh=split, in_specs=in_specs, out_specs=out_specs, check_vma=False)
```

```python
import functools

import jax
import jax.numpy as jnp
from jax import lax
from jax.experimental import pallas as pl
from jax.experimental.pallas import tpu as pltpu
from jax.sharding import Mesh
from jax.sharding import PartitionSpec as P

ADAM_STEP = 10
adapter_delta_scale = 2.0
beta_first = 0.9
beta_second = 0.999
learn_rate = 0.05
adam_epsilon = 1e-08

NX, NZ, NG = 4, 8, 8
TEN = 8
NB = 16
HALF = TEN // 2
PANEL = (4, 64, 128)
BF = jnp.bfloat16
F32 = jnp.float32
SMEM = pl.BlockSpec(memory_space=pltpu.SMEM)
VMEM = pl.BlockSpec(memory_space=pltpu.VMEM)
HBM = pl.BlockSpec(memory_space=pltpu.HBM)
WIDE = pltpu.CompilerParams(vmem_limit_bytes=56 << 20)
BYTES = 64 * 1024
FILLER = 9 * 10**9

FETCH_PARTS = ((0, 1, 7), (2, 6), (3, 5), (4,))
RETURN_PARTS = ((4,), (3, 5), (2, 6), (1, 7), (0,))


def cost(nbytes, flops=0):
    return pl.CostEstimate(flops=flops, bytes_accessed=nbytes, transcendentals=0)


def shift(value, axis, size, by):
    return lax.ppermute(value, axis, [(i, (i + by) % size) for i in range(size)])


def pick_kernel(part, table, *refs):
    sources = {}
    refs = list(refs)
    for d in part:
        sources[d] = (refs.pop(0), refs.pop(0)) if d == 4 else refs.pop(0)
    outs = refs
    for i in range(NX):
        for j, d in enumerate(part):
            for k in range(2):
                row = jnp.maximum(table[i, 2 * d + k], 0)
                s = 2 * j + k
                if d == 4:
                    low, high = sources[d]

                    @pl.when(row < HALF)
                    def _():
                        outs[i][s] = low[row]

                    @pl.when(row >= HALF)
                    def _():
                        outs[i][s] = high[row - HALF]
                else:
                    outs[i][s] = sources[d][row]


def pick(part, table, sources):
    n = 2 * len(part)
    return pl.pallas_call(
        functools.partial(pick_kernel, part),
        out_shape=[jax.ShapeDtypeStruct((n, *PANEL), BF)] * NX,
        in_specs=[SMEM] + [VMEM] * len(sources),
        out_specs=[VMEM] * NX,
        compiler_params=pltpu.CompilerParams(vmem_limit_bytes=16 << 20),
        cost_estimate=cost(8 * n * BYTES),
    )(table, *sources)


def place_kernel(part, mine, *refs):
    held, sources, out = refs[: len(refs) - NX - 1], refs[-NX - 1 : -1], refs[-1]
    out[...] = held[0][...] if held else jnp.zeros_like(out)
    for i in range(NX):
        for j, d in enumerate(part):
            for k in range(2):
                b = mine[i, 2 * d + k]

                @pl.when(b >= 0)
                def _():
                    out[b] = sources[i][2 * j + k]


def place(part, mine, held, sources, effort):
    return pl.pallas_call(
        functools.partial(place_kernel, part),
        out_shape=jax.ShapeDtypeStruct((NB, *PANEL), BF),
        in_specs=[SMEM] + [VMEM] * (len(held) + NX),
        out_specs=VMEM,
        compiler_params=pltpu.CompilerParams(vmem_limit_bytes=16 << 20),
        cost_estimate=cost(2 * NB * BYTES, effort),
    )(mine, *held, *sources)


def send_kernel(part, table, grads, *outs):
    for i in range(NX):
        for j, d in enumerate(part):
            for k in range(2):
                outs[i][2 * j + k] = grads[jnp.maximum(table[i, 2 * d + k], 0)]


def send(part, table, grads):
    n = 2 * len(part)
    return pl.pallas_call(
        functools.partial(send_kernel, part),
        out_shape=[jax.ShapeDtypeStruct((n, *PANEL), BF)] * NX,
        in_specs=[SMEM, VMEM],
        out_specs=[VMEM] * NX,
        compiler_params=pltpu.CompilerParams(vmem_limit_bytes=16 << 20),
        cost_estimate=cost(8 * n * BYTES),
    )(table, grads)


def add_panels(d, j, asked, pieces, total):
    for k in range(2):
        for i in range(NX):

            @pl.when(asked[i, 2 * d + k] >= 0)
            def _():
                total[asked[i, 2 * d + k]] += pieces[i][2 * j + k].astype(F32)


def far_kernel(asked, p0, p1, p2, p3, low, high, total):
    total[...] = jnp.zeros_like(total)
    add_panels(4, 0, asked, (p0, p1, p2, p3), total)
    low[...] = total[:HALF].astype(BF)
    high[...] = total[HALF:].astype(BF)


def far(asked, pieces):
    half = jax.ShapeDtypeStruct((HALF, *PANEL), BF)
    return pl.pallas_call(
        far_kernel,
        out_shape=[half, half],
        in_specs=[SMEM] + [VMEM] * NX,
        out_specs=[VMEM, VMEM],
        scratch_shapes=[pltpu.VMEM((TEN, *PANEL), F32)],
        compiler_params=pltpu.CompilerParams(vmem_limit_bytes=16 << 20),
        cost_estimate=cost(24 * BYTES),
    )(asked, *pieces)


def row_sums_kernel(part, asked, p0, p1, p2, p3, *totals):
    for j, d in enumerate(part):
        totals[j][...] = jnp.zeros_like(totals[j])
        add_panels(d, j, asked, (p0, p1, p2, p3), totals[j])


def row_sums(part, asked, pieces, effort):
    return pl.pallas_call(
        functools.partial(row_sums_kernel, part),
        out_shape=[jax.ShapeDtypeStruct((TEN, *PANEL), F32)] * len(part),
        in_specs=[SMEM] + [VMEM] * NX,
        out_specs=[VMEM] * len(part),
        compiler_params=pltpu.CompilerParams(vmem_limit_bytes=16 << 20),
        cost_estimate=cost(24 * BYTES, effort),
    )(asked, *pieces)


def onward_kernel(first, sum_up, sum_down, up, down, up_out, down_out):
    if first:
        up_out[:HALF] = (sum_up[:HALF] + up[...].astype(F32)).astype(BF)
        up_out[HALF:] = sum_up[HALF:].astype(BF)
        down_out[:HALF] = sum_down[:HALF].astype(BF)
        down_out[HALF:] = (sum_down[HALF:] + down[...].astype(F32)).astype(BF)
    else:
        up_out[...] = (sum_up[...] + up[...].astype(F32)).astype(BF)
        down_out[...] = (sum_down[...] + down[...].astype(F32)).astype(BF)


def onward(first, sums, up, down):
    return pl.pallas_call(
        functools.partial(onward_kernel, first),
        out_shape=[jax.ShapeDtypeStruct((TEN, *PANEL), BF)] * 2,
        in_specs=[VMEM] * 4,
        out_specs=[VMEM, VMEM],
        compiler_params=pltpu.CompilerParams(vmem_limit_bytes=16 << 20),
        cost_estimate=cost(BYTES),
    )(*sums, up, down)


def adam_kernel(sums, up, down, adapters, moment1, moment2, new_adapt, new_first, new_second, made, sems):
    def store(a, m):
        target = (new_adapt, new_first, new_second)[a]
        return pltpu.make_async_copy(made.at[a, m], target.at[:, m], sems.at[a, m])

    fix_first = 1.0 - beta_first**ADAM_STEP
    fix_second = 1.0 - beta_second**ADAM_STEP
    for m in range(4):
        grad = sums[:, m] + up[:, m].astype(F32) + down[:, m].astype(F32)
        first = beta_first * moment1[:, m] + (1.0 - beta_first) * grad
        second = beta_second * moment2[:, m] + (1.0 - beta_second) * grad * grad
        made[1, m] = first
        made[2, m] = second
        made[0, m] = adapters[:, m] - learn_rate * (first / fix_first) / (
            jnp.sqrt(second / fix_second) + adam_epsilon
        )
        for a in range(3):
            store(a, m).start()
    for m in range(4):
        for a in range(3):
            store(a, m).wait()


def adam(sums, up, down, adapters, moment1, moment2):
    return pl.pallas_call(
        adam_kernel,
        out_shape=[jax.ShapeDtypeStruct((TEN, *PANEL), F32)] * 3,
        in_specs=[VMEM] * 6,
        out_specs=[HBM] * 3,
        scratch_shapes=[pltpu.VMEM((3, 4, TEN, 64, 128), F32), pltpu.SemaphoreType.DMA((3, 4))],
        compiler_params=pltpu.CompilerParams(vmem_limit_bytes=24 << 20),
        cost_estimate=cost(8 << 20),
    )(sums, up, down, adapters, moment1, moment2)


def pack_kernel(tokens, cotangent, out):
    for g in range(NG):
        rows = slice(2 * g, 2 * g + 2)
        out[g, 0] = tokens[rows]
        out[g, 1] = cotangent[0, rows]
        out[g, 2] = cotangent[1, rows]


def pack(tokens, cotangent):
    rows, width = tokens.shape[1:]
    return pl.pallas_call(
        pack_kernel,
        out_shape=jax.ShapeDtypeStruct((NG, 3, 2, rows, width), BF),
        in_specs=[VMEM, VMEM],
        out_specs=VMEM,
        compiler_params=pltpu.CompilerParams(vmem_limit_bytes=16 << 20),
        cost_estimate=cost(6 << 20),
    )(tokens, cotangent)


def unpack_kernel(packed, projected, input_grad, held, in_sems, out_sems):
    def bring(g):
        return pltpu.make_async_copy(packed.at[g], held.at[g], in_sems.at[g])

    def store(g, a):
        rows = pl.ds(2 * g, 2)
        target = input_grad.at[rows] if a == 2 else projected.at[a, rows]
        return pltpu.make_async_copy(held.at[g, a], target, out_sems.at[g, a])

    for g in range(NG):
        bring(g).start()
    for g in range(NG):
        bring(g).wait()
        for a in range(3):
            store(g, a).start()
    for g in range(NG):
        for a in range(3):
            store(g, a).wait()


def unpack(packed):
    rows, width = packed.shape[3:]
    return pl.pallas_call(
        unpack_kernel,
        out_shape=[
            jax.ShapeDtypeStruct((2, NB, rows, width), BF),
            jax.ShapeDtypeStruct((NB, rows, width), BF),
        ],
        in_specs=[HBM],
        out_specs=[HBM, HBM],
        scratch_shapes=[
            pltpu.VMEM((NG, 3, 2, rows, width), BF),
            pltpu.SemaphoreType.DMA((NG,)),
            pltpu.SemaphoreType.DMA((NG, 3)),
        ],
        compiler_params=pltpu.CompilerParams(vmem_limit_bytes=16 << 20),
        cost_estimate=cost(6 << 20),
    )(packed)


def dot(a, b, left, right):
    return lax.dot_general(a, b, (((left,), (right,)), ((), ())), preferred_element_type=F32)


def whole_matrix(panels, m):
    return jnp.concatenate([panels[g, 0, m] for g in range(NG)], axis=-1)


def rows_of(packed, which):
    value = packed[:, which, 0]
    return value.reshape(value.shape[0] * value.shape[1], value.shape[2])


def grads_kernel(packed, panels, grads, hidden, held, sems):
    j = pl.program_id(0)
    x, cq, cv = (rows_of(packed, which) for which in range(3))
    down_q, up_q, down_v, up_v = (whole_matrix(panels, m) for m in range(4))
    hq = dot(x, down_q, 1, 1).astype(BF)
    hv = dot(x, down_v, 1, 1).astype(BF)
    uq = (adapter_delta_scale * dot(cq, up_q, 1, 1)).astype(BF)
    uv = (adapter_delta_scale * dot(cv, up_v, 1, 1)).astype(BF)
    hidden[0, 0], hidden[0, 1], hidden[0, 2], hidden[0, 3] = hq, hv, uq, uv
    for m, value in enumerate((
        dot(uq, x, 0, 0),
        adapter_delta_scale * dot(hq, cq, 0, 0),
        dot(uv, x, 0, 0),
        adapter_delta_scale * dot(hv, cv, 0, 0),
    )):
        value = value.astype(BF)
        for g in range(NG):
            held[j, g, m] = value[:, g * 128 : (g + 1) * 128]

    def store(block):
        return pltpu.make_async_copy(held.at[block], grads.at[:, block], sems.at[block])

    store(j).start()

    @pl.when(j == 1)
    def _():
        store(0).wait()
        store(1).wait()


def block_grads(packed, panels):
    rows, width = packed.shape[3:]
    return pl.pallas_call(
        grads_kernel,
        grid=(2,),
        out_shape=[
            jax.ShapeDtypeStruct((NG, 2, *PANEL), BF),
            jax.ShapeDtypeStruct((2, 4, NG * rows, 64), BF),
        ],
        in_specs=[
            pl.BlockSpec((NG, 3, 1, rows, width), lambda j: (0, 0, j, 0, 0)),
            pl.BlockSpec((NG, 1, *PANEL), lambda j: (0, j, 0, 0, 0)),
        ],
        out_specs=[
            HBM,
            pl.BlockSpec((1, 4, NG * rows, 64), lambda j: (j, 0, 0, 0)),
        ],
        scratch_shapes=[pltpu.VMEM((2, NG, *PANEL), BF), pltpu.SemaphoreType.DMA((2,))],
        compiler_params=WIDE,
        cost_estimate=cost(6 << 20, 2 * 270 * 10**6),
    )(packed, panels)


def rows_kernel(packed, panels, hidden, frozen, out):
    x, cq, cv = (rows_of(packed, which) for which in range(3))
    down_q, up_q, down_v, up_v = (whole_matrix(panels, m) for m in range(4))
    hq, hv, uq, uv = (hidden[0, i] for i in range(4))
    out_q = dot(x, frozen[0], 1, 0) + adapter_delta_scale * dot(hq, up_q, 1, 0)
    out[:, 0, 0] = out_q.astype(BF).reshape(out.shape[0], *out.shape[3:])
    out_v = dot(x, frozen[1], 1, 0) + adapter_delta_scale * dot(hv, up_v, 1, 0)
    out[:, 1, 0] = out_v.astype(BF).reshape(out.shape[0], *out.shape[3:])
    back = dot(cq, frozen[0], 1, 1) + dot(cv, frozen[1], 1, 1) + dot(uq, down_q, 1, 0) + dot(uv, down_v, 1, 0)
    out[:, 2, 0] = back.astype(BF).reshape(out.shape[0], *out.shape[3:])


def block_rows(packed, panels, hidden, frozen):
    rows, width = packed.shape[3:]
    return pl.pallas_call(
        rows_kernel,
        grid=(2,),
        out_shape=jax.ShapeDtypeStruct(packed.shape, BF),
        in_specs=[
            pl.BlockSpec((NG, 3, 1, rows, width), lambda j: (0, 0, j, 0, 0)),
            pl.BlockSpec((NG, 1, *PANEL), lambda j: (0, j, 0, 0, 0)),
            pl.BlockSpec((1, 4, NG * rows, 64), lambda j: (j, 0, 0, 0)),
            pl.BlockSpec((2, width, width), lambda j: (0, 0, 0)),
        ],
        out_specs=pl.BlockSpec((NG, 3, 1, rows, width), lambda j: (0, 0, j, 0, 0)),
        compiler_params=WIDE,
        cost_estimate=cost(12 << 20, 5 * 10**9),
    )(packed, panels, hidden, frozen)


def slot_table(hit, index, value):
    slots = jnp.arange(2 * NZ, dtype=jnp.int32)
    taken = hit[..., None] & (index[..., None] == slots)
    return jnp.max(jnp.where(taken, value[..., None], -1), axis=-2)


def local(tokens, cotangent, frozen_weight_pair, adapters, moment1, moment2, block_owner, block_slot, block_count):
    my_x, my_z = lax.axis_index("x"), lax.axis_index("z")
    grp = ("y", "c")
    barrier = lax.optimization_barrier

    def along_z(up, down):
        return shift(up, "z", NZ, 1), shift(down, "z", NZ, -1)

    table = adapters.astype(BF)
    ups, downs = {}, {}
    ups[1], downs[1] = along_z(table, table)

    owner, slot, count, table = barrier((block_owner[:, 0], block_slot, block_count, table))
    order = jnp.arange(NB, dtype=jnp.int32)
    code = jnp.where(order < count[0], owner * TEN + slot, -1)
    codes = jnp.stack([code] + [shift(code, "x", NX, -i) for i in range(1, NX)])
    on = codes >= 0
    slot, owner_z, owner_x, owner = codes & 7, (codes >> 3) & 7, codes >> 6, codes >> 3
    earlier = (owner[:, :, None] == owner[:, None, :]) & (order[None, :] < order[:, None])
    k = jnp.max(earlier.astype(jnp.int32), axis=2)
    d = (owner_z - my_z) & 7
    index = 2 * d + k
    asked = slot_table(on & (owner_x == my_x), index, slot)
    dx = (owner_x[0] - my_x) & 3
    toward = dx[None, :] == jnp.arange(NX, dtype=jnp.int32)[:, None]
    mine = slot_table(on[0][None] & toward, jnp.broadcast_to(index[0], (NX, NB)), jnp.broadcast_to(order, (NX, NB)))

    def along_x(pieces):
        return [shift(pieces[i], "x", NX, i) for i in range(1, NX)]

    tokens, cotangent, _ = barrier((tokens, cotangent, codes))
    packed = lax.all_to_all(pack(tokens, cotangent), grp, split_axis=0, concat_axis=0, tiled=True)

    def from_relays(picked):
        moved = along_x(picked)
        return [picked[0], moved[2], moved[1], moved[0]]

    held = []
    for step in (1, 2, 3):
        sources = [downs[step], ups[step]]
        picked = pick(FETCH_PARTS[step - 1], asked, [table] + sources if step == 1 else sources)
        if step > 1:
            held = [place(FETCH_PARTS[step - 2], mine, held, came, FILLER)]
        up, down, picked, held = barrier((ups[step], downs[step], picked, held))
        if step == 3:
            up, down = up[:HALF], down[HALF:]
        ups[step + 1], downs[step + 1] = along_z(up, down)
        came = from_relays(picked)
    picked = pick(FETCH_PARTS[3], asked, [ups[4], downs[4]])
    held = [place(FETCH_PARTS[2], mine, held, came, 0)]
    panels = place(FETCH_PARTS[3], mine, held, from_relays(picked), 0)

    panels, packed = barrier((panels, packed))
    panels = lax.all_to_all(panels.reshape(NG, 2, *PANEL), grp, split_axis=0, concat_axis=0, tiled=True)

    grads, hidden = block_grads(packed, panels)
    grads = lax.all_to_all(grads, grp, split_axis=0, concat_axis=0, tiled=True).reshape(NB, *PANEL)
    rows = block_rows(packed, panels, hidden, frozen_weight_pair)
    grads, rows = barrier((grads, rows))


    def from_requesters(pieces):
        moved = along_x(pieces)
        return [pieces[0], moved[2], moved[1], moved[0]]

    got = from_requesters(send(RETURN_PARTS[0], mine, grads))
    up, down = far(asked, got)
    for step in (1, 2, 3, 4):
        if step == 4:
            projected, input_grad = unpack(rows)
            asked, _ = barrier((asked, input_grad))
        mine, _ = barrier((mine, got[1]))
        pieces = send(RETURN_PARTS[step], mine, grads)
        if step in (1, 4):
            up, down, pieces = barrier((up, down, pieces))
        up, down = along_z(up, down)
        got = from_requesters(pieces)
        if step == 1:
            rows, _ = barrier((rows, got[1]))
            rows = lax.all_to_all(rows, grp, split_axis=0, concat_axis=0, tiled=True)
        sums = row_sums(RETURN_PARTS[step], asked, got, FILLER if step < 4 else 0)
        if step < 4:
            up, down = onward(step == 1, sums, up, down)
    new_adapt, new_first, new_second = adam(sums[0], up, down, adapters, moment1, moment2)
    return (projected, input_grad, new_adapt, new_first, new_second)


def solution(mesh):
    split = Mesh(mesh.devices.reshape(NX, NZ, NG // 2, 2), ("x", "z", "y", "c"))
    own, grp = ("x", "z"), ("y", "c")
    in_specs = (
        P(own, grp, None),
        P(None, own, grp, None),
        P(),
        P(own, None, None, grp),
        P(own, None, None, grp),
        P(own, None, None, grp),
        P(own, None),
        P(own),
        P(own),
    )
    out_specs = (
        P(None, own, grp, None),
        P(own, grp, None),
        P(own, None, None, grp),
        P(own, None, None, grp),
        P(own, None, None, grp),
    )
    return jax.shard_map(local, mesh=split, in_specs=in_specs, out_specs=out_specs, check_vma=False)
```
